768 devices in a mesh: group: 24 (over z, core), route: 32 (over x, y).
Axes of the slice: x: 4, y: 8, z: 12, core: 2. Of those that a mesh axis runs over, the one named last changes fastest.
Arguments:
- ensemble: bfloat16 [256, 98304], P('route', 'group')
- obs_anom: bfloat16 [256, 98304], P(None, ('group', 'route')), may hold values from -6 to 6
- obs_weight: bfloat16 [256, 98304], P(None, ('group', 'route')), may hold values from -1.5 to 1.5
- taper_table: float32 [16, 128, 128], replicated, may hold values from 0.05 to 1
- pair_obs: int32 [24, 32, 32], P('group', 'route'), may hold values from 0 to 23
- pair_tile: int32 [24, 32, 32], P('group', 'route'), may hold values from 0 to 31
- pair_taper: int32 [24, 32, 32], P('group', 'route'), may hold values from 0 to 15
- pair_count: int32 [24, 32], P('group', 'route'), may hold values from 1 to 32, as said below
Outputs:
- updated: bfloat16 [256, 98304], P('route', 'group')
The draws below stay inside these ranges and needn't reach their ends.
Inputs may be any that keep to these rules, and one draw needn't show every extreme that they name: The first pair_count[g, r] pairs of list (g, r) are live; in every draw some list has exactly 32 live pairs.
All inputs are finite; a program needn't handle non-finite values.
Results may differ from the reference program's by a relative error of at most 0.0075.
Values may be sent and summed in bfloat16 or wider, within the bound.
No kernel may reach another device: no remote copies, remote signals or barrier semaphores. Data moves between devices by JAX's collectives and lax.ppermute only.
A program may use at most 32 MiB of HBM per device.

```python
import math
import jax
import jax.numpy as jnp
from jax import lax

M = 256
TILE = 128
BLOCK = 128
PAIRS = 32
NTAPER = 16
CELLS = 98304
OBS = 98304
N_GROUP = 24
N_ROUTE = 32


def draw_ensemble(key, part):
    first, second, third = jax.random.split(key, 3)
    centre_row = jax.random.uniform(first, (1, CELLS), jnp.float32, -2.0, 2.0)
    spread = jnp.exp(jax.random.uniform(second, (1, CELLS), jnp.float32, math.log(0.3), math.log(1.5)))
    noise = jax.random.normal(third, (M, CELLS), jnp.float32)
    return (centre_row + spread * noise).astype(jnp.bfloat16)


def draw_pair_count(key, part):
    first, second = jax.random.split(key, 2)
    counts = jax.random.randint(first, (N_GROUP, N_ROUTE), 1, PAIRS + 1)
    chosen = jax.random.randint(second, (), 0, N_GROUP * N_ROUTE)
    places = jnp.arange(N_GROUP * N_ROUTE).reshape(N_GROUP, N_ROUTE)
    return jnp.where(places == chosen, PAIRS, counts).astype(jnp.int32)


def set_ends(drawn, stream_key, low, top_value):
    longest = drawn.shape.index(max(drawn.shape))
    spots = []
    for shift in (0, 1):
        where = [jax.random.randint(jax.random.fold_in(stream_key, axis), (), 0, length) for axis, length in enumerate(drawn.shape)]
        where[longest] = (where[longest] + shift) % drawn.shape[longest]
        spots.append(tuple(where))
    return drawn.at[spots[0]].set(low).at[spots[1]].set(top_value)


def levels(stream_key, extent, shards, least, largest):
    def one(position, parts):
        draws = jax.random.uniform(jax.random.fold_in(jax.random.fold_in(stream_key, 6), position), (parts,), jnp.float32, least / len(shards), largest / len(shards))
        return jnp.repeat(jnp.exp(draws), extent[position] // parts).reshape((-1,) + (1,) * (len(extent) - position - 1))

    loudness = one(*shards[0])
    for cut in shards[1:]:
        loudness = loudness * one(*cut)
    return loudness


def normal_values(key, extent, scale, most, cuts=(), dtype=jnp.bfloat16):
    result = jax.random.normal(key, extent, jnp.float32) * scale
    if len(cuts) > 0:
        result = levels(key, extent, cuts, -0.22, 0.18) * result
    return jnp.clip(result, min=-most, max=most).astype(dtype)


def setup_inputs(seed: int = 0) -> dict:
    key_of = jax.random.split(jax.random.key(seed), 9)
    ensemble = draw_ensemble(jax.random.fold_in(key_of[8], 71), 0)
    obs_anom = normal_values(key_of[1], (M, OBS), 1.0, 6.0, ((1, 768),))
    obs_weight = normal_values(key_of[2], (M, OBS), 0.25, 1.5, ((1, 768),))
    taper_table = jnp.clip(jax.random.uniform(key_of[3], (NTAPER, TILE, BLOCK), jnp.float32, 0.05, 1.0), 0.05, 1.0)
    pair_obs = set_ends(jax.random.randint(key_of[4], (N_GROUP, N_ROUTE, PAIRS), 0, N_GROUP), jax.random.fold_in(key_of[4], 1), 0, N_GROUP - 1).astype(jnp.int32)
    pair_tile = set_ends(jax.random.randint(key_of[5], (N_GROUP, N_ROUTE, PAIRS), 0, N_ROUTE), jax.random.fold_in(key_of[5], 1), 0, N_ROUTE - 1).astype(jnp.int32)
    pair_taper = set_ends(jax.random.randint(key_of[6], (N_GROUP, N_ROUTE, PAIRS), 0, NTAPER), jax.random.fold_in(key_of[6], 1), 0, NTAPER - 1).astype(jnp.int32)
    pair_count = draw_pair_count(jax.random.fold_in(key_of[8], 71), 0)
    return dict(ensemble=ensemble, obs_anom=obs_anom, obs_weight=obs_weight, taper_table=taper_table, pair_obs=pair_obs, pair_tile=pair_tile, pair_taper=pair_taper, pair_count=pair_count)


def reference(ensemble, obs_anom, obs_weight, taper_table, pair_obs, pair_tile, pair_taper, pair_count):
    ensemble_f = ensemble.astype(jnp.float32)
    centre_row = jnp.sum(ensemble_f, axis=0) / M
    anomaly = (ensemble_f - centre_row[None, :]).astype(jnp.bfloat16)
    panels = anomaly.reshape(M, N_GROUP, N_ROUTE, TILE)
    y_blocks = obs_anom.reshape(M, N_GROUP, N_ROUTE, BLOCK)
    w_blocks = obs_weight.reshape(M, N_GROUP, N_ROUTE, BLOCK)

    def one_group(group_index):
        group_panel = jnp.take(panels, group_index, axis=1)

        def one_source(route_index):
            column_y = jnp.take(y_blocks, route_index, axis=2)
            column_w = jnp.take(w_blocks, route_index, axis=2)
            pair_blocks = pair_obs[group_index, route_index]
            pair_tiles = pair_tile[group_index, route_index]
            pair_kinds = pair_taper[group_index, route_index]
            live_count = pair_count[group_index, route_index]
            a_pairs = jnp.take(group_panel, pair_tiles, axis=1).astype(jnp.float32)
            y_pairs = jnp.take(column_y, pair_blocks, axis=1).astype(jnp.float32)
            w_pairs = jnp.take(column_w, pair_blocks, axis=1).astype(jnp.float32)
            cross = jnp.einsum("mqi,mqj->qij", a_pairs, y_pairs)
            is_live = jnp.arange(PAIRS) < live_count
            tapers = jnp.take(taper_table, pair_kinds, axis=0)
            gain_blocks = jnp.where(is_live[:, None, None], tapers * cross / (M - 1), 0.0).astype(jnp.bfloat16)
            weighted = jnp.einsum("mqj,qij->qmi", w_pairs, gain_blocks.astype(jnp.float32))
            summed = jax.ops.segment_sum(weighted, pair_tiles, num_segments=N_ROUTE)
            partial_sum = jnp.transpose(summed, (1, 0, 2))
            return partial_sum.astype(jnp.bfloat16)

        partials = lax.map(one_source, jnp.arange(N_ROUTE))
        return jnp.sum(partials.astype(jnp.float32), axis=0)

    updates = lax.map(one_group, jnp.arange(N_GROUP))
    update = jnp.transpose(updates, (1, 0, 2, 3)).reshape(M, N_GROUP * N_ROUTE * TILE)
    return (ensemble_f + update).astype(jnp.bfloat16)
```

```python
import jax
import jax.numpy as jnp
from jax import lax
from jax.experimental import pallas as pl
from jax.experimental.pallas import tpu as pltpu
from jax.sharding import Mesh, PartitionSpec as P

Z, CORE, X, Y = 12, 2, 4, 8
UNROLL = 4


def pair_kernel(
    tile_ref, obs_ref, kind_ref, count_ref, core_ref,
    panel_ref, own_ref, other_ref, taper_ref, out_ref, anom_ref, acc_ref,
):
    tiles, members, width = acc_ref.shape

    @pl.loop(0, tiles)
    def _(t):
        cells = panel_ref[:, pl.ds(pl.multiple_of(t * width, width), width)].astype(jnp.float32)
        centre = jnp.sum(cells, axis=0, keepdims=True) * (1.0 / members)
        anom_ref[t] = (cells - centre).astype(jnp.bfloat16)
        acc_ref[t] = jnp.zeros((members, width), jnp.float32)

    count = count_ref[0]
    core = core_ref[0]

    @pl.loop(0, lax.div(count + (UNROLL - 1), UNROLL))
    def _(step):
        terms = []
        for u in range(UNROLL):
            q = step * UNROLL + u
            t, j, k = tile_ref[q], obs_ref[q], kind_ref[q]
            z = lax.shift_right_logical(j, 1)
            mine = (j & 1) == core
            y_low = jnp.where(mine, own_ref[z, 0:128], other_ref[z, 0:128])
            y_high = jnp.where(mine, own_ref[z, 128:256], other_ref[z, 128:256])
            w = jnp.where(mine, own_ref[z, 256:512], other_ref[z, 256:512])
            y = jnp.concatenate([y_low, y_high], axis=1)
            cross = jnp.dot(y, anom_ref[t], preferred_element_type=jnp.float32)
            gain = jnp.where(q < count, taper_ref[k] * cross, 0.0).astype(jnp.bfloat16)
            terms.append((t, jnp.dot(w, gain, preferred_element_type=jnp.float32)))
        for t, term in terms:
            acc_ref[t] += term

    @pl.loop(0, tiles)
    def _(t):
        out_ref[:, pl.ds(pl.multiple_of(t * width, width), width)] = acc_ref[t].astype(jnp.bfloat16)


def on_device(
    ensemble, obs_anom, obs_weight, taper_table, pair_obs, pair_tile, pair_taper, pair_count
):
    rows, cells = ensemble.shape
    members = rows * X * Y
    width = obs_anom.shape[1]
    half = members // 2
    blocks = jnp.concatenate([obs_anom[:half].T, obs_anom[half:].T, obs_weight], axis=0)
    own = lax.all_gather(blocks, "z", axis=0)
    other = lax.ppermute(own, "core", [(0, 1), (1, 0)])
    part = lax.all_to_all(jnp.broadcast_to(ensemble[None], (Y, rows, cells)), "y", 0, 0, tiled=True)
    part = part.reshape(1, Y * rows, cells)
    panel = lax.all_to_all(jnp.broadcast_to(part, (X, Y * rows, cells)), "x", 0, 0, tiled=True)
    panel = panel.reshape(members, cells)
    tapers = jnp.swapaxes(taper_table, 1, 2) * (1.0 / (members - 1))
    smem = pl.BlockSpec(memory_space=pltpu.SMEM)
    vmem = pl.BlockSpec(memory_space=pltpu.VMEM)
    partial = pl.pallas_call(
        pair_kernel,
        out_shape=jax.ShapeDtypeStruct((members, cells), jnp.bfloat16),
        in_specs=[smem] * 5 + [vmem] * 4,
        out_specs=vmem,
        scratch_shapes=[
            pltpu.VMEM((cells // width, members, width), jnp.bfloat16),
            pltpu.VMEM((cells // width, members, width), jnp.float32),
        ],
        compiler_params=pltpu.CompilerParams(vmem_limit_bytes=40 * 2**20),
        name="pairs",
    )(
        pair_tile[0, 0], pair_obs[0, 0], pair_taper[0, 0], pair_count[0],
        lax.axis_index("core").reshape(1), panel, own, other, tapers,
    )
    sent = lax.all_to_all(partial.reshape(X, Y * rows, cells), "x", 0, 0, tiled=True)
    summed = jnp.sum(sent.astype(jnp.float32), axis=0).astype(jnp.bfloat16)
    sent = lax.all_to_all(summed.reshape(Y, rows, cells), "y", 0, 0, tiled=True)
    update = jnp.sum(sent.astype(jnp.float32), axis=0)
    return (ensemble.astype(jnp.float32) + update).astype(jnp.bfloat16)


def solution(mesh):
    fine = Mesh(mesh.devices.reshape(Z, CORE, X, Y), ("z", "core", "x", "y"))
    group, route = ("z", "core"), ("x", "y")
    placed = (
        P(route, group),
        P(None, group + route),
        P(None, group + route),
        P(),
        P(group, route, None),
        P(group, route, None),
        P(group, route, None),
        P(group, route),
    )
    return jax.shard_map(
        on_device, mesh=fine, in_specs=placed, out_specs=P(route, group), check_vma=False
    )
```

```python
import jax
import jax.numpy as jnp
from jax import lax
from jax.experimental import pallas as pl
from jax.experimental.pallas import tpu as pltpu
from jax.sharding import Mesh, PartitionSpec as P

Z, CORE, X, YH, YL = 12, 2, 4, 4, 2
Y = YH * YL
UNROLL = 4


def anomaly_kernel(panel_ref, anom_ref):
    tiles, width, members = anom_ref.shape

    @pl.loop(0, tiles)
    def _(t):
        cells = panel_ref[:, pl.ds(pl.multiple_of(t * width, width), width)].astype(jnp.float32)
        centre = jnp.sum(cells, axis=0, keepdims=True) * (1.0 / members)
        anom_ref[t] = (cells - centre).T.astype(jnp.bfloat16)


def pair_kernel(
    tile_ref, obs_ref, kind_ref, count_ref, anom_ref, blocks_ref, taper_ref, out_ref, acc_ref
):
    tiles, members, width = acc_ref.shape

    @pl.loop(0, tiles)
    def _(t):
        acc_ref[t] = jnp.zeros((members, width), jnp.float32)

    count = count_ref[0]

    @pl.loop(0, lax.div(count + (UNROLL - 1), UNROLL))
    def _(step):
        terms = []
        for u in range(UNROLL):
            q = step * UNROLL + u
            t, j, k = tile_ref[q], obs_ref[q], kind_ref[q]
            cross = jnp.dot(
                anom_ref[t], blocks_ref[j, 0:members], preferred_element_type=jnp.float32
            )
            scaled = taper_ref[k] * cross * (1.0 / (members - 1))
            gain = jnp.where(q < count, scaled, 0.0).astype(jnp.bfloat16)
            term = lax.dot_general(
                blocks_ref[j, members : 2 * members],
                gain,
                (((1,), (1,)), ((), ())),
                preferred_element_type=jnp.float32,
            )
            terms.append((t, term))
        for t, term in terms:
            acc_ref[t] += term

    @pl.loop(0, tiles)
    def _(t):
        out_ref[:, pl.ds(pl.multiple_of(t * width, width), width)] = acc_ref[t].astype(jnp.bfloat16)


def on_device(
    ensemble, obs_anom, obs_weight, taper_table, pair_obs, pair_tile, pair_taper, pair_count
):
    rows, cells = ensemble.shape
    members = rows * X * Y
    width = obs_anom.shape[1]
    tiles = cells // width
    weight = obs_weight.reshape(X, YH, YL, rows, width).transpose(0, 2, 1, 3, 4)
    blocks = jnp.concatenate([obs_anom, weight.reshape(members, width)], axis=0)
    blocks = lax.all_gather(blocks, ("z", "core"), axis=0)
    y_axes = ("yh", "yl")
    part = lax.all_to_all(
        jnp.broadcast_to(ensemble[None], (Y, rows, cells)), y_axes, 0, 0, tiled=True
    )
    part = part.reshape(1, Y * rows, cells)
    panel = lax.all_to_all(jnp.broadcast_to(part, (X, Y * rows, cells)), "x", 0, 0, tiled=True)
    smem = pl.BlockSpec(memory_space=pltpu.SMEM)
    vmem = pl.BlockSpec(memory_space=pltpu.VMEM)
    anom = pl.pallas_call(
        anomaly_kernel,
        out_shape=jax.ShapeDtypeStruct((tiles, width, members), jnp.bfloat16),
        in_specs=[vmem],
        out_specs=vmem,
        compiler_params=pltpu.CompilerParams(vmem_limit_bytes=24 * 2**20),
        name="anomalies",
    )(panel.reshape(members, cells))
    partial = pl.pallas_call(
        pair_kernel,
        out_shape=jax.ShapeDtypeStruct((members, cells), jnp.bfloat16),
        in_specs=[smem] * 4 + [vmem] * 3,
        out_specs=vmem,
        scratch_shapes=[pltpu.VMEM((tiles, members, width), jnp.float32)],
        compiler_params=pltpu.CompilerParams(vmem_limit_bytes=40 * 2**20),
        name="pairs",
    )(pair_tile[0, 0], pair_obs[0, 0], pair_taper[0, 0], pair_count[0], anom, blocks, taper_table)
    sent = partial.reshape(X * YL, YH * rows, cells)
    sent = lax.all_to_all(sent, ("x", "yl"), 0, 0, tiled=True)
    summed = jnp.sum(sent.astype(jnp.float32), axis=0).astype(jnp.bfloat16)
    sent = lax.all_to_all(summed.reshape(YH, rows, cells), "yh", 0, 0, tiled=True)
    update = jnp.sum(sent.astype(jnp.float32), axis=0)
    return (ensemble.astype(jnp.float32) + update).astype(jnp.bfloat16)


def solution(mesh):
    fine = Mesh(
        mesh.devices.reshape(Z, CORE, X, YH, YL), ("z", "core", "x", "yh", "yl")
    )
    group, route = ("z", "core"), ("x", "yh", "yl")
    placed = (
        P(route, group),
        P(None, group + route),
        P(None, group + route),
        P(),
        P(group, route, None),
        P(group, route, None),
        P(group, route, None),
        P(group, route),
    )
    return jax.shard_map(
        on_device, mesh=fine, in_specs=placed, out_specs=P(route, group), check_vma=False
    )
```

```python
import jax
import jax.numpy as jnp
from jax import lax
from jax.experimental import pallas as pl
from jax.experimental.pallas import tpu as pltpu
from jax.sharding import Mesh, PartitionSpec as P

Z, CORE, X, YH, YL = 12, 2, 4, 4, 2
Y = YH * YL
UNROLL = 4


def anomaly_kernel(panel_ref, anom_ref):
    tiles, members, width = anom_ref.shape

    @pl.loop(0, tiles, unroll=2)
    def _(t):
        cells = panel_ref[:, pl.ds(pl.multiple_of(t * width, width), width)].astype(jnp.float32)
        centre = jnp.sum(cells, axis=0, keepdims=True) * (1.0 / members)
        anom_ref[t] = (cells - centre).astype(jnp.bfloat16)


def pair_kernel(
    tile_ref, obs_ref, kind_ref, count_ref, anom_ref, blocks_ref, taper_ref, out_ref,
    acc_ref, held_ref, sems,
):
    tiles, members, width = acc_ref.shape
    count = count_ref[0]
    steps = lax.div(count + (UNROLL - 1), UNROLL)

    def fetch(q):
        return pltpu.make_async_copy(blocks_ref.at[obs_ref[q]], held_ref.at[q], sems.at[q])

    @pl.loop(0, steps * UNROLL)
    def _(q):
        fetch(q).start()

    @pl.loop(0, tiles)
    def _(t):
        acc_ref[t] = jnp.zeros((members, width), jnp.float32)

    @pl.loop(0, steps)
    def _(step):
        for u in range(UNROLL):
            fetch(step * UNROLL + u).wait()
        terms = []
        for u in range(UNROLL):
            q = step * UNROLL + u
            t, k = tile_ref[q], kind_ref[q]
            y = jnp.concatenate([held_ref[q, 0:128], held_ref[q, 128:256]], axis=1)
            cross = jnp.dot(y, anom_ref[t], preferred_element_type=jnp.float32)
            gain = jnp.where(q < count, taper_ref[k] * cross, 0.0).astype(jnp.bfloat16)
            w = held_ref[q, members : 2 * members]
            terms.append((t, jnp.dot(w, gain, preferred_element_type=jnp.float32)))
        for t, term in terms:
            acc_ref[t] += term

    @pl.loop(0, tiles, unroll=2)
    def _(t):
        out_ref[:, pl.ds(pl.multiple_of(t * width, width), width)] = acc_ref[t].astype(jnp.bfloat16)


def on_device(
    ensemble, obs_anom, obs_weight, taper_table, pair_obs, pair_tile, pair_taper, pair_count
):
    rows, cells = ensemble.shape
    members = rows * X * Y
    width = obs_anom.shape[1]
    tiles = cells // width
    pairs = pair_tile.shape[2]
    half = members // 2
    weight = obs_weight.reshape(X, YH, YL, rows, width).transpose(0, 2, 1, 3, 4)
    blocks = jnp.concatenate(
        [obs_anom[:half].T, obs_anom[half:].T, weight.reshape(members, width)], axis=0
    )
    blocks = lax.all_gather(blocks, ("z", "core"), axis=0)
    y_axes = ("yh", "yl")
    part = lax.all_to_all(
        jnp.broadcast_to(ensemble[None], (Y, rows, cells)), y_axes, 0, 0, tiled=True
    )
    part = part.reshape(1, Y * rows, cells)
    panel = lax.all_to_all(jnp.broadcast_to(part, (X, Y * rows, cells)), "x", 0, 0, tiled=True)
    tapers = jnp.swapaxes(taper_table, 1, 2) * (1.0 / (members - 1))
    smem = pl.BlockSpec(memory_space=pltpu.SMEM)
    vmem = pl.BlockSpec(memory_space=pltpu.VMEM)
    anom = pl.pallas_call(
        anomaly_kernel,
        out_shape=jax.ShapeDtypeStruct((tiles, members, width), jnp.bfloat16),
        in_specs=[vmem],
        out_specs=vmem,
        compiler_params=pltpu.CompilerParams(vmem_limit_bytes=10 * 2**20),
        name="anomalies",
    )(panel.reshape(members, cells))
    partial = pl.pallas_call(
        pair_kernel,
        out_shape=jax.ShapeDtypeStruct((members, cells), jnp.bfloat16),
        in_specs=[smem] * 4 + [vmem, pl.BlockSpec(memory_space=pltpu.HBM), vmem],
        out_specs=vmem,
        scratch_shapes=[
            pltpu.VMEM((tiles, members, width), jnp.float32),
            pltpu.VMEM((pairs, 2 * members, width), jnp.bfloat16),
            pltpu.SemaphoreType.DMA((pairs,)),
        ],
        compiler_params=pltpu.CompilerParams(vmem_limit_bytes=47 * 2**20),
        name="pairs",
    )(pair_tile[0, 0], pair_obs[0, 0], pair_taper[0, 0], pair_count[0], anom, blocks, tapers)
    sent = partial.reshape(X * YL, YH * rows, cells)
    sent = lax.all_to_all(sent, ("x", "yl"), 0, 0, tiled=True)
    summed = jnp.sum(sent.astype(jnp.float32), axis=0).astype(jnp.bfloat16)
    sent = lax.all_to_all(summed.reshape(YH, rows, cells), "yh", 0, 0, tiled=True)
    update = jnp.sum(sent.astype(jnp.float32), axis=0)
    return (ensemble.astype(jnp.float32) + update).astype(jnp.bfloat16)


def solution(mesh):
    fine = Mesh(
        mesh.devices.reshape(Z, CORE, X, YH, YL), ("z", "core", "x", "yh", "yl")
    )
    group, route = ("z", "core"), ("x", "yh", "yl")
    placed = (
        P(route, group),
        P(None, group + route),
        P(None, group + route),
        P(),
        P(group, route, None),
        P(group, route, None),
        P(group, route, None),
        P(group, route),
    )
    return jax.shard_map(
        on_device, mesh=fine, in_specs=placed, out_specs=P(route, group), check_vma=False
    )
```

```python
import jax
import jax.numpy as jnp
from jax import lax
from jax.experimental import pallas as pl
from jax.experimental.pallas import tpu as pltpu
from jax.sharding import Mesh, PartitionSpec as P

Z, CORE, X, YH, YL = 12, 2, 4, 4, 2
Y = YH * YL
UNROLL = 16


def anomaly_kernel(panel_ref, anom_ref):
    tiles, members, width = anom_ref.shape

    @pl.loop(0, tiles, unroll=2)
    def _(t):
        cells = panel_ref[:, pl.ds(pl.multiple_of(t * width, width), width)].astype(jnp.float32)
        centre = jnp.sum(cells, axis=0, keepdims=True) * (1.0 / members)
        anom_ref[t] = (cells - centre).astype(jnp.bfloat16)


def pair_kernel(
    tile_ref, obs_ref, kind_ref, count_ref, anom_ref, blocks_ref, taper_ref, out_ref,
    acc_ref, held_ref, sems, gain_ref,
):
    tiles, members, width = acc_ref.shape
    count = count_ref[0]
    steps = lax.div(count + (UNROLL - 1), UNROLL)

    y_copy = pltpu.make_async_copy(
        blocks_ref.at[:, 0:members], held_ref.at[:, 0:members], sems.at[0]
    )
    w_copy = pltpu.make_async_copy(
        blocks_ref.at[:, members : 2 * members], held_ref.at[:, members : 2 * members], sems.at[1]
    )
    y_copy.start()
    w_copy.start()

    @pl.loop(0, tiles, unroll=4)
    def _(t):
        acc_ref[t] = jnp.zeros((members, width), jnp.float32)

    y_copy.wait()

    @pl.loop(0, steps)
    def _(step):
        for u in range(UNROLL):
            q = step * UNROLL + u
            y = jnp.concatenate([held_ref[obs_ref[q], 0:128], held_ref[obs_ref[q], 128:256]], axis=1)
            cross = jnp.dot(y, anom_ref[tile_ref[q]], preferred_element_type=jnp.float32)
            gain = jnp.where(q < count, taper_ref[kind_ref[q]] * cross, 0.0)
            gain_ref[q] = gain.astype(jnp.bfloat16)

    w_copy.wait()

    @pl.loop(0, steps)
    def _(step):
        for u in range(UNROLL):
            q = step * UNROLL + u
            w = held_ref[obs_ref[q], members : 2 * members]
            acc_ref[tile_ref[q]] += jnp.dot(w, gain_ref[q], preferred_element_type=jnp.float32)

    @pl.loop(0, tiles, unroll=4)
    def _(t):
        out_ref[:, pl.ds(pl.multiple_of(t * width, width), width)] = acc_ref[t].astype(jnp.bfloat16)


def on_device(
    ensemble, obs_anom, obs_weight, taper_table, pair_obs, pair_tile, pair_taper, pair_count
):
    rows, cells = ensemble.shape
    members = rows * X * Y
    width = obs_anom.shape[1]
    tiles = cells // width
    pairs = pair_tile.shape[2]
    half = members // 2
    weight = obs_weight.reshape(X, YH, YL, rows, width).transpose(0, 2, 1, 3, 4)
    blocks = jnp.concatenate(
        [obs_anom[:half].T, obs_anom[half:].T, weight.reshape(members, width)], axis=0
    )
    blocks = lax.all_gather(blocks, ("z", "core"), axis=0)
    y_axes = ("yh", "yl")
    part = lax.all_to_all(
        jnp.broadcast_to(ensemble[None], (Y, rows, cells)), y_axes, 0, 0, tiled=True
    )
    part = part.reshape(1, Y * rows, cells)
    panel = lax.all_to_all(jnp.broadcast_to(part, (X, Y * rows, cells)), "x", 0, 0, tiled=True)
    tapers = jnp.swapaxes(taper_table, 1, 2) * (1.0 / (members - 1))
    smem = pl.BlockSpec(memory_space=pltpu.SMEM)
    vmem = pl.BlockSpec(memory_space=pltpu.VMEM)
    anom = pl.pallas_call(
        anomaly_kernel,
        out_shape=jax.ShapeDtypeStruct((tiles, members, width), jnp.bfloat16),
        in_specs=[vmem],
        out_specs=vmem,
        compiler_params=pltpu.CompilerParams(vmem_limit_bytes=10 * 2**20),
        name="anomalies",
    )(panel.reshape(members, cells))
    partial = pl.pallas_call(
        pair_kernel,
        out_shape=jax.ShapeDtypeStruct((members, cells), jnp.bfloat16),
        in_specs=[smem] * 4 + [vmem, pl.BlockSpec(memory_space=pltpu.HBM), vmem],
        out_specs=vmem,
        scratch_shapes=[
            pltpu.VMEM((tiles, members, width), jnp.float32),
            pltpu.VMEM(blocks.shape, jnp.bfloat16),
            pltpu.SemaphoreType.DMA((2,)),
            pltpu.VMEM((pairs, width, width), jnp.bfloat16),
        ],
        compiler_params=pltpu.CompilerParams(vmem_limit_bytes=47 * 2**20),
        name="pairs",
    )(pair_tile[0, 0], pair_obs[0, 0], pair_taper[0, 0], pair_count[0], anom, blocks, tapers)
    sent = partial.reshape(X * YL, YH * rows, cells)
    sent = lax.all_to_all(sent, ("x", "yl"), 0, 0, tiled=True)
    summed = jnp.sum(sent.astype(jnp.float32), axis=0).astype(jnp.bfloat16)
    sent = lax.all_to_all(summed.reshape(YH, rows, cells), "yh", 0, 0, tiled=True)
    update = jnp.sum(sent.astype(jnp.float32), axis=0)
    return (ensemble.astype(jnp.float32) + update).astype(jnp.bfloat16)


def solution(mesh):
    fine = Mesh(
        mesh.devices.reshape(Z, CORE, X, YH, YL), ("z", "core", "x", "yh", "yl")
    )
    group, route = ("z", "core"), ("x", "yh", "yl")
    placed = (
        P(route, group),
        P(None, group + route),
        P(None, group + route),
        P(),
        P(group, route, None),
        P(group, route, None),
        P(group, route, None),
        P(group, route),
    )
    return jax.shard_map(
        on_device, mesh=fine, in_specs=placed, out_specs=P(route, group), check_vma=False
    )
```

```python
import jax
import jax.numpy as jnp
from jax import lax
from jax.experimental import pallas as pl
from jax.experimental.pallas import tpu as pltpu
from jax.sharding import Mesh, PartitionSpec as P

Z, CORE, X, YH, YL = 12, 2, 4, 4, 2
Y = YH * YL
UNROLL = 16


def pair_kernel(
    tile_ref, obs_ref, kind_ref, count_ref, anom_ref, blocks_ref, taper_ref, out_ref,
    acc_ref, held_ref, sems, gain_ref,
):
    tiles, members, width = acc_ref.shape
    count = count_ref[0]
    steps = lax.div(count + (UNROLL - 1), UNROLL)

    y_copy = pltpu.make_async_copy(
        blocks_ref.at[:, 0:members], held_ref.at[:, 0:members], sems.at[0]
    )
    w_copy = pltpu.make_async_copy(
        blocks_ref.at[:, members : 2 * members], held_ref.at[:, members : 2 * members], sems.at[1]
    )
    y_copy.start()
    w_copy.start()

    @pl.loop(0, tiles, unroll=4)
    def _(t):
        acc_ref[t] = jnp.zeros((members, width), jnp.float32)

    y_copy.wait()

    @pl.loop(0, steps)
    def _(step):
        for u in range(UNROLL):
            q = step * UNROLL + u
            y = jnp.concatenate([held_ref[obs_ref[q], 0:128], held_ref[obs_ref[q], 128:256]], axis=1)
            start = pl.multiple_of(tile_ref[q] * width, width)
            anom = anom_ref[:, pl.ds(start, width)]
            cross = jnp.dot(y, anom, preferred_element_type=jnp.float32)
            gain = jnp.where(q < count, taper_ref[kind_ref[q]] * cross, 0.0)
            gain_ref[q] = gain.astype(jnp.bfloat16)

    w_copy.wait()

    @pl.loop(0, steps)
    def _(step):
        for u in range(UNROLL):
            q = step * UNROLL + u
            w = held_ref[obs_ref[q], members : 2 * members]
            acc_ref[tile_ref[q]] += jnp.dot(w, gain_ref[q], preferred_element_type=jnp.float32)

    @pl.loop(0, tiles, unroll=4)
    def _(t):
        out_ref[:, pl.ds(pl.multiple_of(t * width, width), width)] = acc_ref[t].astype(jnp.bfloat16)


def on_device(
    ensemble, obs_anom, obs_weight, taper_table, pair_obs, pair_tile, pair_taper, pair_count
):
    rows, cells = ensemble.shape
    members = rows * X * Y
    width = obs_anom.shape[1]
    tiles = cells // width
    pairs = pair_tile.shape[2]
    half = members // 2

    def reorder(array):
        split = array.reshape(X, YH, YL, rows, width)
        return split.transpose(0, 2, 1, 3, 4).reshape(members, width)

    anomalies = reorder(obs_anom)
    blocks = jnp.concatenate(
        [anomalies[:half].T, anomalies[half:].T, reorder(obs_weight)], axis=0
    )
    blocks = lax.all_gather(blocks, ("z", "core"), axis=0)
    part = jnp.broadcast_to(ensemble[None], (YH, rows, cells))
    part = lax.all_to_all(part, "yh", 0, 0, tiled=True).reshape(1, YH * rows, cells)
    panel = jnp.broadcast_to(part, (X * YL, YH * rows, cells))
    panel = lax.all_to_all(panel, ("x", "yl"), 0, 0, tiled=True)
    panel = panel.reshape(members, cells).astype(jnp.float32)
    centre = jnp.sum(panel, axis=0, keepdims=True) * (1.0 / members)
    anom = (panel - centre).astype(jnp.bfloat16)
    tapers = jnp.swapaxes(taper_table, 1, 2) * (1.0 / (members - 1))
    smem = pl.BlockSpec(memory_space=pltpu.SMEM)
    vmem = pl.BlockSpec(memory_space=pltpu.VMEM)
    partial = pl.pallas_call(
        pair_kernel,
        out_shape=jax.ShapeDtypeStruct((members, cells), jnp.bfloat16),
        in_specs=[smem] * 4 + [vmem, pl.BlockSpec(memory_space=pltpu.HBM), vmem],
        out_specs=vmem,
        scratch_shapes=[
            pltpu.VMEM((tiles, members, width), jnp.float32),
            pltpu.VMEM(blocks.shape, jnp.bfloat16),
            pltpu.SemaphoreType.DMA((2,)),
            pltpu.VMEM((pairs, width, width), jnp.bfloat16),
        ],
        compiler_params=pltpu.CompilerParams(vmem_limit_bytes=47 * 2**20),
        name="pairs",
    )(pair_tile[0, 0], pair_obs[0, 0], pair_taper[0, 0], pair_count[0], anom, blocks, tapers)
    sent = partial.reshape(X * YL, YH * rows, cells)
    sent = lax.all_to_all(sent, ("x", "yl"), 0, 0, tiled=True)
    summed = jnp.sum(sent.astype(jnp.float32), axis=0).astype(jnp.bfloat16)
    sent = lax.all_to_all(summed.reshape(YH, rows, cells), "yh", 0, 0, tiled=True)
    update = jnp.sum(sent.astype(jnp.float32), axis=0)
    return (ensemble.astype(jnp.float32) + update).astype(jnp.bfloat16)


def solution(mesh):
    fine = Mesh(
        mesh.devices.reshape(Z, CORE, X, YH, YL), ("z", "core", "x", "yh", "yl")
    )
    group, route = ("z", "core"), ("x", "yh", "yl")
    placed = (
        P(route, group),
        P(None, group + route),
        P(None, group + route),
        P(),
        P(group, route, None),
        P(group, route, None),
        P(group, route, None),
        P(group, route),
    )
    return jax.shard_map(
        on_device, mesh=fine, in_specs=placed, out_specs=P(route, group), check_vma=False
    )
```

```python
import jax
import jax.numpy as jnp
from jax import lax
from jax.experimental import pallas as pl
from jax.experimental.pallas import tpu as pltpu
from jax.sharding import Mesh, PartitionSpec as P

Z, CORE, XH, XL, YH, YL = 12, 2, 2, 2, 4, 2
X, Y = XH * XL, YH * YL
FAR = ("xh", "yh")
PLANES = ("core", "xh", "xl", "yh", "yl")


def neighbour_blocks():
    groups = []
    for core in range(CORE):
        for bx in range(XH):
            for by in range(YH):
                xs = sorted(((2 * bx + core + a) % X for a in range(2)), key=lambda x: x % 2)
                ys = sorted(((2 * by + core + b) % Y for b in range(2)), key=lambda y: y % 2)
                groups.append([(core * X + x) * Y + y for x in xs for y in ys])
    return groups


def near_exchange(array):
    return lax.all_to_all(
        array, PLANES, 0, 0, axis_index_groups=neighbour_blocks(), tiled=True
    )


def far_exchange(array):
    return lax.all_to_all(array, FAR, 0, 0, tiled=True)
UNROLL = 16


def pair_kernel(
    tile_ref, obs_ref, kind_ref, count_ref, anom_ref, blocks_ref, taper_ref, out_ref,
    acc_ref, held_ref, sems, gain_ref,
):
    tiles, members, width = acc_ref.shape
    count = count_ref[0]
    steps = lax.div(count + (UNROLL - 1), UNROLL)

    y_copy = pltpu.make_async_copy(
        blocks_ref.at[:, 0:members], held_ref.at[:, 0:members], sems.at[0]
    )
    w_copy = pltpu.make_async_copy(
        blocks_ref.at[:, members : 2 * members], held_ref.at[:, members : 2 * members], sems.at[1]
    )
    y_copy.start()
    w_copy.start()

    @pl.loop(0, tiles, unroll=4)
    def _(t):
        acc_ref[t] = jnp.zeros((members, width), jnp.float32)

    y_copy.wait()

    @pl.loop(0, steps)
    def _(step):
        for u in range(UNROLL):
            q = step * UNROLL + u
            y = jnp.concatenate([held_ref[obs_ref[q], 0:128], held_ref[obs_ref[q], 128:256]], axis=1)
            start = pl.multiple_of(tile_ref[q] * width, width)
            anom = anom_ref[:, pl.ds(start, width)]
            cross = jnp.dot(y, anom, preferred_element_type=jnp.float32)
            gain = jnp.where(q < count, taper_ref[kind_ref[q]] * cross, 0.0)
            gain_ref[q] = gain.astype(jnp.bfloat16)

    w_copy.wait()

    @pl.loop(0, steps)
    def _(step):
        for u in range(UNROLL):
            q = step * UNROLL + u
            w = held_ref[obs_ref[q], members : 2 * members]
            acc_ref[tile_ref[q]] += jnp.dot(w, gain_ref[q], preferred_element_type=jnp.float32)

    @pl.loop(0, tiles, unroll=4)
    def _(t):
        out_ref[:, pl.ds(pl.multiple_of(t * width, width), width)] = acc_ref[t].astype(jnp.bfloat16)


def on_device(
    ensemble, obs_anom, obs_weight, taper_table, pair_obs, pair_tile, pair_taper, pair_count
):
    rows, cells = ensemble.shape
    members = rows * X * Y
    width = obs_anom.shape[1]
    tiles = cells // width
    pairs = pair_tile.shape[2]
    half = members // 2

    def reorder(array):
        split = array.reshape(XH, XL, YH, YL, rows, width)
        return split.transpose(1, 3, 0, 2, 4, 5).reshape(members, width)

    anomalies = reorder(obs_anom)
    blocks = jnp.concatenate(
        [anomalies[:half].T, anomalies[half:].T, reorder(obs_weight)], axis=0
    )
    blocks = lax.all_gather(blocks, ("z", "core"), axis=0)
    part = far_exchange(jnp.broadcast_to(ensemble[None], (XH * YH, rows, cells)))
    part = part.reshape(1, XH * YH * rows, cells)
    panel = near_exchange(jnp.broadcast_to(part, (XL * YL, XH * YH * rows, cells)))
    panel = panel.reshape(members, cells).astype(jnp.float32)
    centre = jnp.sum(panel, axis=0, keepdims=True) * (1.0 / members)
    anom = (panel - centre).astype(jnp.bfloat16)
    tapers = jnp.swapaxes(taper_table, 1, 2) * (1.0 / (members - 1))
    smem = pl.BlockSpec(memory_space=pltpu.SMEM)
    vmem = pl.BlockSpec(memory_space=pltpu.VMEM)
    partial = pl.pallas_call(
        pair_kernel,
        out_shape=jax.ShapeDtypeStruct((members, cells), jnp.bfloat16),
        in_specs=[smem] * 4 + [vmem, pl.BlockSpec(memory_space=pltpu.HBM), vmem],
        out_specs=vmem,
        scratch_shapes=[
            pltpu.VMEM((tiles, members, width), jnp.float32),
            pltpu.VMEM(blocks.shape, jnp.bfloat16),
            pltpu.SemaphoreType.DMA((2,)),
            pltpu.VMEM((pairs, width, width), jnp.bfloat16),
        ],
        compiler_params=pltpu.CompilerParams(vmem_limit_bytes=47 * 2**20),
        name="pairs",
    )(pair_tile[0, 0], pair_obs[0, 0], pair_taper[0, 0], pair_count[0], anom, blocks, tapers)
    sent = near_exchange(partial.reshape(XL * YL, XH * YH * rows, cells))
    summed = jnp.sum(sent.astype(jnp.float32), axis=0).astype(jnp.bfloat16)
    sent = far_exchange(summed.reshape(XH * YH, rows, cells))
    update = jnp.sum(sent.astype(jnp.float32), axis=0)
    return (ensemble.astype(jnp.float32) + update).astype(jnp.bfloat16)


def solution(mesh):
    fine = Mesh(
        mesh.devices.reshape(Z, CORE, XH, XL, YH, YL), ("z", "core", "xh", "xl", "yh", "yl")
    )
    group, route = ("z", "core"), ("xh", "xl", "yh", "yl")
    placed = (
        P(route, group),
        P(None, group + route),
        P(None, group + route),
        P(),
        P(group, route, None),
        P(group, route, None),
        P(group, route, None),
        P(group, route),
    )
    return jax.shard_map(
        on_device, mesh=fine, in_specs=placed, out_specs=P(route, group), check_vma=False
    )
```

```python
import jax
import jax.numpy as jnp
from jax import lax
from jax.experimental import pallas as pl
from jax.experimental.pallas import tpu as pltpu
from jax.sharding import Mesh, PartitionSpec as P

Z, CORE, XH, XL, YH, YL = 12, 2, 2, 2, 4, 2
X, Y = XH * XL, YH * YL
FAR = ("xh", "yh")
PLANES = ("core", "xh", "xl", "yh", "yl")


def neighbour_blocks():
    groups = []
    for core in range(CORE):
        for bx in range(XH):
            for by in range(YH):
                xs = sorted(((2 * bx + core + a) % X for a in range(2)), key=lambda x: x % 2)
                ys = sorted(((2 * by + core + b) % Y for b in range(2)), key=lambda y: y % 2)
                groups.append([(core * X + x) * Y + y for x in xs for y in ys])
    return groups


HX, KX = (0, 1, 1, 0), (0, 0, 1, 1)
HY, KY, LY = (0, 1, 1, 0, 0, 1, 1, 0), (0, 0, 1, 0, 1, 1, 0, 1), (0, 0, 0, 1, 0, 1, 1, 1)


def place(core, u, v):
    return (u + core) % X * Y + (v + core) % Y


def route_groups(same, order):
    groups = []
    for core in range(CORE):
        found = {}
        for u in range(X):
            for v in range(Y):
                member = (order(u, v), core * X * Y + place(core, u, v))
                found.setdefault(same(u, v), []).append(member)
        groups += [[device for _, device in sorted(found[key])] for key in sorted(found)]
    return groups


def first_groups():
    return route_groups(lambda u, v: (u // 2, v // 2), lambda u, v: (HX[u], HY[v]))


def second_groups():
    return route_groups(
        lambda u, v: ((u + 1) % X // 2, (v + 1) % Y // 2), lambda u, v: (KX[u], KY[v])
    )


def third_groups():
    return route_groups(lambda u, v: (u, HY[v], KY[v]), lambda u, v: LY[v])


def row_order(core):
    keys = []
    for u in range(X):
        for v in range(Y):
            keys.append(((HX[u], HY[v], KX[u], KY[v], LY[v]), place(core, u, v)))
    return [owner for _, owner in sorted(keys)]


def summed_exchange(array, groups):
    parts = array.reshape(len(groups[0]), array.shape[0] // len(groups[0]), array.shape[1])
    parts = lax.all_to_all(parts, PLANES, 0, 0, axis_index_groups=groups, tiled=True)
    return jnp.sum(parts.astype(jnp.float32), axis=0)


def near_exchange(array):
    return lax.all_to_all(
        array, PLANES, 0, 0, axis_index_groups=neighbour_blocks(), tiled=True
    )


def far_exchange(array):
    return lax.all_to_all(array, FAR, 0, 0, tiled=True)
UNROLL = 16


def pair_kernel(
    tile_ref, obs_ref, kind_ref, count_ref, core_ref, anom_ref, blocks_ref, taper_ref, out_ref,
    acc_ref, held_ref, sems, gain_ref,
):
    tiles, members, width = acc_ref.shape
    count = count_ref[0]
    steps = lax.div(count + (UNROLL - 1), UNROLL)

    y_copy = pltpu.make_async_copy(
        blocks_ref.at[:, 0:members], held_ref.at[:, 0:members], sems.at[0]
    )
    w_copy = pltpu.make_async_copy(
        blocks_ref.at[:, members : 2 * members], held_ref.at[:, members : 2 * members], sems.at[1]
    )
    y_copy.start()
    w_copy.start()

    @pl.loop(0, tiles, unroll=4)
    def _(t):
        acc_ref[t] = jnp.zeros((members, width), jnp.float32)

    y_copy.wait()

    @pl.loop(0, steps)
    def _(step):
        for u in range(UNROLL):
            q = step * UNROLL + u
            y = jnp.concatenate([held_ref[obs_ref[q], 0:128], held_ref[obs_ref[q], 128:256]], axis=1)
            start = pl.multiple_of(tile_ref[q] * width, width)
            anom = anom_ref[:, pl.ds(start, width)]
            cross = jnp.dot(y, anom, preferred_element_type=jnp.float32)
            gain = jnp.where(q < count, taper_ref[kind_ref[q]] * cross, 0.0)
            gain_ref[q] = gain.astype(jnp.bfloat16)

    w_copy.wait()

    @pl.loop(0, steps)
    def _(step):
        for u in range(UNROLL):
            q = step * UNROLL + u
            w = held_ref[obs_ref[q], members : 2 * members]
            acc_ref[tile_ref[q]] += jnp.dot(w, gain_ref[q], preferred_element_type=jnp.float32)

    rows = members // (X * Y)
    for core in range(CORE):
        order = row_order(core)

        @pl.when(core_ref[0] == core)
        def _():
            @pl.loop(0, tiles, unroll=2)
            def _(t):
                total = acc_ref[t]
                total = jnp.concatenate([total[rows * r : rows * (r + 1)] for r in order], axis=0)
                cells = pl.ds(pl.multiple_of(t * width, width), width)
                out_ref[:, cells] = total.astype(jnp.bfloat16)


def on_device(
    ensemble, obs_anom, obs_weight, taper_table, pair_obs, pair_tile, pair_taper, pair_count
):
    rows, cells = ensemble.shape
    members = rows * X * Y
    width = obs_anom.shape[1]
    tiles = cells // width
    pairs = pair_tile.shape[2]
    half = members // 2

    def reorder(array):
        split = array.reshape(XH, XL, YH, YL, rows, width)
        return split.transpose(1, 3, 0, 2, 4, 5).reshape(members, width)

    anomalies = reorder(obs_anom)
    blocks = jnp.concatenate(
        [anomalies[:half].T, anomalies[half:].T, obs_weight], axis=0
    )
    blocks = lax.all_gather(blocks, ("z", "core"), axis=0)
    part = far_exchange(jnp.broadcast_to(ensemble[None], (XH * YH, rows, cells)))
    part = part.reshape(1, XH * YH * rows, cells)
    panel = near_exchange(jnp.broadcast_to(part, (XL * YL, XH * YH * rows, cells)))
    panel = panel.reshape(members, cells).astype(jnp.float32)
    centre = jnp.sum(panel, axis=0, keepdims=True) * (1.0 / members)
    anom = (panel - centre).astype(jnp.bfloat16)
    tapers = jnp.swapaxes(taper_table, 1, 2) * (1.0 / (members - 1))
    smem = pl.BlockSpec(memory_space=pltpu.SMEM)
    vmem = pl.BlockSpec(memory_space=pltpu.VMEM)
    partial = pl.pallas_call(
        pair_kernel,
        out_shape=jax.ShapeDtypeStruct((members, cells), jnp.bfloat16),
        in_specs=[smem] * 5 + [vmem, pl.BlockSpec(memory_space=pltpu.HBM), vmem],
        out_specs=vmem,
        scratch_shapes=[
            pltpu.VMEM((tiles, members, width), jnp.float32),
            pltpu.VMEM(blocks.shape, jnp.bfloat16),
            pltpu.SemaphoreType.DMA((2,)),
            pltpu.VMEM((pairs, width, width), jnp.bfloat16),
        ],
        compiler_params=pltpu.CompilerParams(vmem_limit_bytes=47 * 2**20),
        name="pairs",
    )(
        pair_tile[0, 0], pair_obs[0, 0], pair_taper[0, 0], pair_count[0],
        lax.axis_index("core").reshape(1), anom, blocks, tapers,
    )
    summed = summed_exchange(partial, first_groups()).astype(jnp.bfloat16)
    summed = summed_exchange(summed, second_groups()).astype(jnp.bfloat16)
    update = summed_exchange(summed, third_groups())
    return (ensemble.astype(jnp.float32) + update).astype(jnp.bfloat16)


def solution(mesh):
    fine = Mesh(
        mesh.devices.reshape(Z, CORE, XH, XL, YH, YL), ("z", "core", "xh", "xl", "yh", "yl")
    )
    group, route = ("z", "core"), ("xh", "xl", "yh", "yl")
    placed = (
        P(route, group),
        P(None, group + route),
        P(None, group + route),
        P(),
        P(group, route, None),
        P(group, route, None),
        P(group, route, None),
        P(group, route),
    )
    return jax.shard_map(
        on_device, mesh=fine, in_specs=placed, out_specs=P(route, group), check_vma=False
    )
```

```python
import jax
import jax.numpy as jnp
from jax import lax
from jax.experimental import pallas as pl
from jax.experimental.pallas import tpu as pltpu
from jax.sharding import Mesh, PartitionSpec as P

Z, CORE, XH, XL, YH, YL = 12, 2, 2, 2, 4, 2
X, Y = XH * XL, YH * YL
FAR = ("xh", "yh")
PLANES = ("core", "xh", "xl", "yh", "yl")


def neighbour_blocks():
    groups = []
    for core in range(CORE):
        for bx in range(XH):
            for by in range(YH):
                xs = sorted(((2 * bx + core + a) % X for a in range(2)), key=lambda x: x % 2)
                ys = sorted(((2 * by + core + b) % Y for b in range(2)), key=lambda y: y % 2)
                groups.append([(core * X + x) * Y + y for x in xs for y in ys])
    return groups


HX, KX = (0, 1, 1, 0), (0, 0, 1, 1)
HY, KY, LY = (0, 1, 1, 0, 0, 1, 1, 0), (0, 0, 1, 0, 1, 1, 0, 1), (0, 0, 0, 1, 0, 1, 1, 1)


def place(core, u, v):
    return (u + core) % X * Y + (v + core) % Y


def route_groups(same, order):
    groups = []
    for core in range(CORE):
        found = {}
        for u in range(X):
            for v in range(Y):
                member = (order(u, v), core * X * Y + place(core, u, v))
                found.setdefault(same(u, v), []).append(member)
        groups += [[device for _, device in sorted(found[key])] for key in sorted(found)]
    return groups


def first_groups():
    return route_groups(lambda u, v: (u // 2, v // 2), lambda u, v: (HX[u], HY[v]))


def second_groups():
    return route_groups(lambda u, v: (HX[u], HY[v]), lambda u, v: (KX[u], KY[v], LY[v]))


def row_order(core):
    keys = []
    for u in range(X):
        for v in range(Y):
            keys.append(((HX[u], HY[v], KX[u], KY[v], LY[v]), place(core, u, v)))
    return [owner for _, owner in sorted(keys)]


def summed_exchange(array, groups):
    parts = array.reshape(len(groups[0]), array.shape[0] // len(groups[0]), array.shape[1])
    parts = lax.all_to_all(parts, PLANES, 0, 0, axis_index_groups=groups, tiled=True)
    return jnp.sum(parts.astype(jnp.float32), axis=0)


def near_exchange(array):
    return lax.all_to_all(
        array, PLANES, 0, 0, axis_index_groups=neighbour_blocks(), tiled=True
    )


def far_exchange(array):
    return lax.all_to_all(array, FAR, 0, 0, tiled=True)
UNROLL = 16


def pair_kernel(
    tile_ref, obs_ref, kind_ref, count_ref, core_ref, anom_ref, blocks_ref, taper_ref, out_ref,
    acc_ref, held_ref, sems, gain_ref,
):
    tiles, members, width = acc_ref.shape
    count = count_ref[0]
    steps = lax.div(count + (UNROLL - 1), UNROLL)

    y_copy = pltpu.make_async_copy(
        blocks_ref.at[:, 0:members], held_ref.at[:, 0:members], sems.at[0]
    )
    w_copy = pltpu.make_async_copy(
        blocks_ref.at[:, members : 2 * members], held_ref.at[:, members : 2 * members], sems.at[1]
    )
    y_copy.start()
    w_copy.start()

    @pl.loop(0, tiles, unroll=4)
    def _(t):
        acc_ref[t] = jnp.zeros((members, width), jnp.float32)

    y_copy.wait()

    @pl.loop(0, steps)
    def _(step):
        for u in range(UNROLL):
            q = step * UNROLL + u
            y = jnp.concatenate([held_ref[obs_ref[q], 0:128], held_ref[obs_ref[q], 128:256]], axis=1)
            start = pl.multiple_of(tile_ref[q] * width, width)
            anom = anom_ref[:, pl.ds(start, width)]
            cross = jnp.dot(y, anom, preferred_element_type=jnp.float32)
            gain = jnp.where(q < count, taper_ref[kind_ref[q]] * cross, 0.0)
            gain_ref[q] = gain.astype(jnp.bfloat16)

    w_copy.wait()

    @pl.loop(0, steps)
    def _(step):
        for u in range(UNROLL):
            q = step * UNROLL + u
            w = held_ref[obs_ref[q], members : 2 * members]
            acc_ref[tile_ref[q]] += jnp.dot(w, gain_ref[q], preferred_element_type=jnp.float32)

    rows = members // (X * Y)
    for core in range(CORE):
        order = row_order(core)

        @pl.when(core_ref[0] == core)
        def _():
            @pl.loop(0, tiles, unroll=2)
            def _(t):
                total = acc_ref[t]
                total = jnp.concatenate([total[rows * r : rows * (r + 1)] for r in order], axis=0)
                cells = pl.ds(pl.multiple_of(t * width, width), width)
                out_ref[:, cells] = total.astype(jnp.bfloat16)


def on_device(
    ensemble, obs_anom, obs_weight, taper_table, pair_obs, pair_tile, pair_taper, pair_count
):
    rows, cells = ensemble.shape
    members = rows * X * Y
    width = obs_anom.shape[1]
    tiles = cells // width
    pairs = pair_tile.shape[2]
    half = members // 2

    def reorder(array):
        split = array.reshape(XH, XL, YH, YL, rows, width)
        return split.transpose(1, 3, 0, 2, 4, 5).reshape(members, width)

    anomalies = reorder(obs_anom)
    blocks = jnp.concatenate(
        [anomalies[:half].T, anomalies[half:].T, obs_weight], axis=0
    )
    blocks = lax.all_gather(blocks, ("z", "core"), axis=0)
    part = far_exchange(jnp.broadcast_to(ensemble[None], (XH * YH, rows, cells)))
    part = part.reshape(1, XH * YH * rows, cells)
    panel = near_exchange(jnp.broadcast_to(part, (XL * YL, XH * YH * rows, cells)))
    panel = panel.reshape(members, cells).astype(jnp.float32)
    centre = jnp.sum(panel, axis=0, keepdims=True) * (1.0 / members)
    anom = (panel - centre).astype(jnp.bfloat16)
    tapers = jnp.swapaxes(taper_table, 1, 2) * (1.0 / (members - 1))
    smem = pl.BlockSpec(memory_space=pltpu.SMEM)
    vmem = pl.BlockSpec(memory_space=pltpu.VMEM)
    partial = pl.pallas_call(
        pair_kernel,
        out_shape=jax.ShapeDtypeStruct((members, cells), jnp.bfloat16),
        in_specs=[smem] * 5 + [vmem, pl.BlockSpec(memory_space=pltpu.HBM), vmem],
        out_specs=vmem,
        scratch_shapes=[
            pltpu.VMEM((tiles, members, width), jnp.float32),
            pltpu.VMEM(blocks.shape, jnp.bfloat16),
            pltpu.SemaphoreType.DMA((2,)),
            pltpu.VMEM((pairs, width, width), jnp.bfloat16),
        ],
        compiler_params=pltpu.CompilerParams(vmem_limit_bytes=47 * 2**20),
        name="pairs",
    )(
        pair_tile[0, 0], pair_obs[0, 0], pair_taper[0, 0], pair_count[0],
        lax.axis_index("core").reshape(1), anom, blocks, tapers,
    )
    summed = summed_exchange(partial, first_groups()).astype(jnp.bfloat16)
    update = summed_exchange(summed, second_groups())
    return (ensemble.astype(jnp.float32) + update).astype(jnp.bfloat16)


def solution(mesh):
    fine = Mesh(
        mesh.devices.reshape(Z, CORE, XH, XL, YH, YL), ("z", "core", "xh", "xl", "yh", "yl")
    )
    group, route = ("z", "core"), ("xh", "xl", "yh", "yl")
    placed = (
        P(route, group),
        P(None, group + route),
        P(None, group + route),
        P(),
        P(group, route, None),
        P(group, route, None),
        P(group, route, None),
        P(group, route),
    )
    return jax.shard_map(
        on_device, mesh=fine, in_specs=placed, out_specs=P(route, group), check_vma=False
    )
```

```python
import jax
import jax.numpy as jnp
from jax import lax
from jax.experimental import pallas as pl
from jax.experimental.pallas import tpu as pltpu
from jax.sharding import Mesh, PartitionSpec as P

Z, CORE, XH, XL, YH, YL = 12, 2, 2, 2, 4, 2
X, Y = XH * XL, YH * YL
FAR = ("xh", "yh")
PLANES = ("core", "xh", "xl", "yh", "yl")


def neighbour_blocks():
    groups = []
    for core in range(CORE):
        for bx in range(XH):
            for by in range(YH):
                xs = sorted(((2 * bx + core + a) % X for a in range(2)), key=lambda x: x % 2)
                ys = sorted(((2 * by + core + b) % Y for b in range(2)), key=lambda y: y % 2)
                groups.append([(core * X + x) * Y + y for x in xs for y in ys])
    return groups


HX, KX = (0, 1, 1, 0), (0, 0, 1, 1)
HY, KY, LY = (0, 1, 1, 0, 0, 1, 1, 0), (0, 0, 1, 0, 1, 1, 0, 1), (0, 0, 0, 1, 0, 1, 1, 1)


def place(core, u, v):
    return (u + 1 - core) % X * Y + (v + core) % Y


def route_groups(same, order):
    groups = []
    for core in range(CORE):
        found = {}
        for u in range(X):
            for v in range(Y):
                member = (order(u, v), core * X * Y + place(core, u, v))
                found.setdefault(same(u, v), []).append(member)
        groups += [[device for _, device in sorted(found[key])] for key in sorted(found)]
    return groups


def first_groups():
    return route_groups(lambda u, v: (u // 2, v // 2), lambda u, v: (HX[u], HY[v]))


def second_groups():
    return route_groups(
        lambda u, v: ((u + 1) % X // 2, (v + 1) % Y // 2), lambda u, v: (KX[u], KY[v])
    )


def third_groups():
    return route_groups(lambda u, v: (u, HY[v], KY[v]), lambda u, v: LY[v])


def row_order(core):
    keys = []
    for u in range(X):
        for v in range(Y):
            keys.append(((HX[u], HY[v], KX[u], KY[v], LY[v]), place(core, u, v)))
    return [owner for _, owner in sorted(keys)]


def summed_exchange(array, groups):
    parts = array.reshape(len(groups[0]), array.shape[0] // len(groups[0]), array.shape[1])
    parts = lax.all_to_all(parts, PLANES, 0, 0, axis_index_groups=groups, tiled=True)
    return jnp.sum(parts.astype(jnp.float32), axis=0)


def near_exchange(array):
    return lax.all_to_all(
        array, PLANES, 0, 0, axis_index_groups=neighbour_blocks(), tiled=True
    )


def far_exchange(array):
    return lax.all_to_all(array, FAR, 0, 0, tiled=True)
UNROLL = 16


def pair_kernel(
    tile_ref, obs_ref, kind_ref, count_ref, core_ref, anom_ref, blocks_ref, taper_ref, out_ref,
    acc_ref, held_ref, sems, gain_ref,
):
    tiles, members, width = acc_ref.shape
    count = count_ref[0]
    steps = lax.div(count + (UNROLL - 1), UNROLL)

    y_copy = pltpu.make_async_copy(
        blocks_ref.at[:, 0:members], held_ref.at[:, 0:members], sems.at[0]
    )
    w_copy = pltpu.make_async_copy(
        blocks_ref.at[:, members : 2 * members], held_ref.at[:, members : 2 * members], sems.at[1]
    )
    y_copy.start()
    w_copy.start()

    @pl.loop(0, tiles, unroll=4)
    def _(t):
        acc_ref[t] = jnp.zeros((members, width), jnp.float32)

    y_copy.wait()

    @pl.loop(0, steps)
    def _(step):
        for u in range(UNROLL):
            q = step * UNROLL + u
            y = jnp.concatenate([held_ref[obs_ref[q], 0:128], held_ref[obs_ref[q], 128:256]], axis=1)
            start = pl.multiple_of(tile_ref[q] * width, width)
            anom = anom_ref[:, pl.ds(start, width)]
            cross = jnp.dot(y, anom, preferred_element_type=jnp.float32)
            gain = jnp.where(q < count, taper_ref[kind_ref[q]] * cross, 0.0)
            gain_ref[q] = gain.astype(jnp.bfloat16)

    w_copy.wait()

    @pl.loop(0, steps)
    def _(step):
        for u in range(UNROLL):
            q = step * UNROLL + u
            w = held_ref[obs_ref[q], members : 2 * members]
            acc_ref[tile_ref[q]] += jnp.dot(w, gain_ref[q], preferred_element_type=jnp.float32)

    rows = members // (X * Y)
    for core in range(CORE):
        order = row_order(core)

        @pl.when(core_ref[0] == core)
        def _():
            @pl.loop(0, tiles, unroll=2)
            def _(t):
                total = acc_ref[t]
                total = jnp.concatenate([total[rows * r : rows * (r + 1)] for r in order], axis=0)
                cells = pl.ds(pl.multiple_of(t * width, width), width)
                out_ref[:, cells] = total.astype(jnp.bfloat16)


def on_device(
    ensemble, obs_anom, obs_weight, taper_table, pair_obs, pair_tile, pair_taper, pair_count
):
    rows, cells = ensemble.shape
    members = rows * X * Y
    width = obs_anom.shape[1]
    tiles = cells // width
    pairs = pair_tile.shape[2]
    half = members // 2

    def reorder(array):
        split = array.reshape(XH, XL, YH, YL, rows, width)
        return split.transpose(1, 3, 0, 2, 4, 5).reshape(members, width)

    anomalies = reorder(obs_anom)
    blocks = jnp.concatenate(
        [anomalies[:half].T, anomalies[half:].T, obs_weight], axis=0
    )
    blocks = lax.all_gather(blocks, ("z", "core"), axis=0)
    part = far_exchange(jnp.broadcast_to(ensemble[None], (XH * YH, rows, cells)))
    part = part.reshape(1, XH * YH * rows, cells)
    panel = near_exchange(jnp.broadcast_to(part, (XL * YL, XH * YH * rows, cells)))
    panel = panel.reshape(members, cells).astype(jnp.float32)
    centre = jnp.sum(panel, axis=0, keepdims=True) * (1.0 / members)
    anom = (panel - centre).astype(jnp.bfloat16)
    tapers = jnp.swapaxes(taper_table, 1, 2) * (1.0 / (members - 1))
    smem = pl.BlockSpec(memory_space=pltpu.SMEM)
    vmem = pl.BlockSpec(memory_space=pltpu.VMEM)
    partial = pl.pallas_call(
        pair_kernel,
        out_shape=jax.ShapeDtypeStruct((members, cells), jnp.bfloat16),
        in_specs=[smem] * 5 + [vmem, pl.BlockSpec(memory_space=pltpu.HBM), vmem],
        out_specs=vmem,
        scratch_shapes=[
            pltpu.VMEM((tiles, members, width), jnp.float32),
            pltpu.VMEM(blocks.shape, jnp.bfloat16),
            pltpu.SemaphoreType.DMA((2,)),
            pltpu.VMEM((pairs, width, width), jnp.bfloat16),
        ],
        compiler_params=pltpu.CompilerParams(vmem_limit_bytes=47 * 2**20),
        name="pairs",
    )(
        pair_tile[0, 0], pair_obs[0, 0], pair_taper[0, 0], pair_count[0],
        lax.axis_index("core").reshape(1), anom, blocks, tapers,
    )
    summed = summed_exchange(partial, first_groups()).astype(jnp.bfloat16)
    summed = summed_exchange(summed, second_groups()).astype(jnp.bfloat16)
    update = summed_exchange(summed, third_groups())
    return (ensemble.astype(jnp.float32) + update).astype(jnp.bfloat16)


def solution(mesh):
    fine = Mesh(
        mesh.devices.reshape(Z, CORE, XH, XL, YH, YL), ("z", "core", "xh", "xl", "yh", "yl")
    )
    group, route = ("z", "core"), ("xh", "xl", "yh", "yl")
    placed = (
        P(route, group),
        P(None, group + route),
        P(None, group + route),
        P(),
        P(group, route, None),
        P(group, route, None),
        P(group, route, None),
        P(group, route),
    )
    return jax.shard_map(
        on_device, mesh=fine, in_specs=placed, out_specs=P(route, group), check_vma=False
    )
```

```python
import jax
import jax.numpy as jnp
from jax import lax
from jax.experimental import pallas as pl
from jax.experimental.pallas import tpu as pltpu
from jax.sharding import Mesh, PartitionSpec as P

Z, CORE, XH, XL, YH, YL = 12, 2, 2, 2, 4, 2
X, Y = XH * XL, YH * YL
FAR = ("xh", "yh")
PLANES = ("core", "xh", "xl", "yh", "yl")


def neighbour_blocks():
    groups = []
    for core in range(CORE):
        for bx in range(XH):
            for by in range(YH):
                xs = sorted(((2 * bx + core + a) % X for a in range(2)), key=lambda x: x % 2)
                ys = sorted(((2 * by + core + b) % Y for b in range(2)), key=lambda y: y % 2)
                groups.append([(core * X + x) * Y + y for x in xs for y in ys])
    return groups


HX, KX = (0, 1, 1, 0), (0, 0, 1, 1)
HY, KY, LY = (0, 1, 1, 0, 0, 1, 1, 0), (0, 0, 1, 0, 1, 1, 0, 1), (0, 0, 0, 1, 0, 1, 1, 1)


def place(core, u, v):
    return (u + core) % X * Y + (v + 1 - core) % Y


def route_groups(same, order):
    groups = []
    for core in range(CORE):
        found = {}
        for u in range(X):
            for v in range(Y):
                member = (order(u, v), core * X * Y + place(core, u, v))
                found.setdefault(same(u, v), []).append(member)
        groups += [[device for _, device in sorted(found[key])] for key in sorted(found)]
    return groups


def first_groups():
    return route_groups(lambda u, v: (u // 2, v // 2), lambda u, v: (HX[u], HY[v]))


def second_groups():
    return route_groups(
        lambda u, v: ((u + 1) % X // 2, (v + 1) % Y // 2), lambda u, v: (KX[u], KY[v])
    )


def third_groups():
    return route_groups(lambda u, v: (u, HY[v], KY[v]), lambda u, v: LY[v])


def row_order(core):
    keys = []
    for u in range(X):
        for v in range(Y):
            keys.append(((HX[u], HY[v], KX[u], KY[v], LY[v]), place(core, u, v)))
    return [owner for _, owner in sorted(keys)]


def summed_exchange(array, groups):
    parts = array.reshape(len(groups[0]), array.shape[0] // len(groups[0]), array.shape[1])
    parts = lax.all_to_all(parts, PLANES, 0, 0, axis_index_groups=groups, tiled=True)
    return jnp.sum(parts.astype(jnp.float32), axis=0)


def near_exchange(array):
    return lax.all_to_all(
        array, PLANES, 0, 0, axis_index_groups=neighbour_blocks(), tiled=True
    )


def far_exchange(array):
    return lax.all_to_all(array, FAR, 0, 0, tiled=True)
UNROLL = 16


def pair_kernel(
    tile_ref, obs_ref, kind_ref, count_ref, core_ref, anom_ref, blocks_ref, taper_ref, out_ref,
    acc_ref, held_ref, sems, gain_ref,
):
    tiles, members, width = acc_ref.shape
    count = count_ref[0]
    steps = lax.div(count + (UNROLL - 1), UNROLL)

    y_copy = pltpu.make_async_copy(
        blocks_ref.at[:, 0:members], held_ref.at[:, 0:members], sems.at[0]
    )
    w_copy = pltpu.make_async_copy(
        blocks_ref.at[:, members : 2 * members], held_ref.at[:, members : 2 * members], sems.at[1]
    )
    y_copy.start()
    w_copy.start()

    @pl.loop(0, tiles, unroll=4)
    def _(t):
        acc_ref[t] = jnp.zeros((members, width), jnp.float32)

    y_copy.wait()

    @pl.loop(0, steps)
    def _(step):
        for u in range(UNROLL):
            q = step * UNROLL + u
            y = jnp.concatenate([held_ref[obs_ref[q], 0:128], held_ref[obs_ref[q], 128:256]], axis=1)
            start = pl.multiple_of(tile_ref[q] * width, width)
            anom = anom_ref[:, pl.ds(start, width)]
            cross = jnp.dot(y, anom, preferred_element_type=jnp.float32)
            gain = jnp.where(q < count, taper_ref[kind_ref[q]] * cross, 0.0)
            gain_ref[q] = gain.astype(jnp.bfloat16)

    w_copy.wait()

    @pl.loop(0, steps)
    def _(step):
        for u in range(UNROLL):
            q = step * UNROLL + u
            w = held_ref[obs_ref[q], members : 2 * members]
            acc_ref[tile_ref[q]] += jnp.dot(w, gain_ref[q], preferred_element_type=jnp.float32)

    rows = members // (X * Y)
    for core in range(CORE):
        order = row_order(core)

        @pl.when(core_ref[0] == core)
        def _():
            @pl.loop(0, tiles, unroll=2)
            def _(t):
                total = acc_ref[t]
                total = jnp.concatenate([total[rows * r : rows * (r + 1)] for r in order], axis=0)
                cells = pl.ds(pl.multiple_of(t * width, width), width)
                out_ref[:, cells] = total.astype(jnp.bfloat16)


def on_device(
    ensemble, obs_anom, obs_weight, taper_table, pair_obs, pair_tile, pair_taper, pair_count
):
    rows, cells = ensemble.shape
    members = rows * X * Y
    width = obs_anom.shape[1]
    tiles = cells // width
    pairs = pair_tile.shape[2]
    half = members // 2

    def reorder(array):
        split = array.reshape(XH, XL, YH, YL, rows, width)
        return split.transpose(1, 3, 0, 2, 4, 5).reshape(members, width)

    anomalies = reorder(obs_anom)
    blocks = jnp.concatenate(
        [anomalies[:half].T, anomalies[half:].T, obs_weight], axis=0
    )
    blocks = lax.all_gather(blocks, ("z", "core"), axis=0)
    part = far_exchange(jnp.broadcast_to(ensemble[None], (XH * YH, rows, cells)))
    part = part.reshape(1, XH * YH * rows, cells)
    panel = near_exchange(jnp.broadcast_to(part, (XL * YL, XH * YH * rows, cells)))
    panel = panel.reshape(members, cells).astype(jnp.float32)
    centre = jnp.sum(panel, axis=0, keepdims=True) * (1.0 / members)
    anom = (panel - centre).astype(jnp.bfloat16)
    tapers = jnp.swapaxes(taper_table, 1, 2) * (1.0 / (members - 1))
    smem = pl.BlockSpec(memory_space=pltpu.SMEM)
    vmem = pl.BlockSpec(memory_space=pltpu.VMEM)
    partial = pl.pallas_call(
        pair_kernel,
        out_shape=jax.ShapeDtypeStruct((members, cells), jnp.bfloat16),
        in_specs=[smem] * 5 + [vmem, pl.BlockSpec(memory_space=pltpu.HBM), vmem],
        out_specs=vmem,
        scratch_shapes=[
            pltpu.VMEM((tiles, members, width), jnp.float32),
            pltpu.VMEM(blocks.shape, jnp.bfloat16),
            pltpu.SemaphoreType.DMA((2,)),
            pltpu.VMEM((pairs, width, width), jnp.bfloat16),
        ],
        compiler_params=pltpu.CompilerParams(vmem_limit_bytes=47 * 2**20),
        name="pairs",
    )(
        pair_tile[0, 0], pair_obs[0, 0], pair_taper[0, 0], pair_count[0],
        lax.axis_index("core").reshape(1), anom, blocks, tapers,
    )
    summed = summed_exchange(partial, first_groups()).astype(jnp.bfloat16)
    summed = summed_exchange(summed, second_groups()).astype(jnp.bfloat16)
    update = summed_exchange(summed, third_groups())
    return (ensemble.astype(jnp.float32) + update).astype(jnp.bfloat16)


def solution(mesh):
    fine = Mesh(
        mesh.devices.reshape(Z, CORE, XH, XL, YH, YL), ("z", "core", "xh", "xl", "yh", "yl")
    )
    group, route = ("z", "core"), ("xh", "xl", "yh", "yl")
    placed = (
        P(route, group),
        P(None, group + route),
        P(None, group + route),
        P(),
        P(group, route, None),
        P(group, route, None),
        P(group, route, None),
        P(group, route),
    )
    return jax.shard_map(
        on_device, mesh=fine, in_specs=placed, out_specs=P(route, group), check_vma=False
    )
```

```python
import jax
import jax.numpy as jnp
from jax import lax
from jax.experimental import pallas as pl
from jax.experimental.pallas import tpu as pltpu
from jax.sharding import Mesh, PartitionSpec as P

Z, CORE, XH, XL, YH, YL = 12, 2, 2, 2, 4, 2
X, Y = XH * XL, YH * YL
FAR = ("xh", "yh")
PLANES = ("core", "xh", "xl", "yh", "yl")


def neighbour_blocks():
    groups = []
    for core in range(CORE):
        for bx in range(XH):
            for by in range(YH):
                xs = sorted(((2 * bx + core + a) % X for a in range(2)), key=lambda x: x % 2)
                ys = sorted(((2 * by + core + b) % Y for b in range(2)), key=lambda y: y % 2)
                groups.append([(core * X + x) * Y + y for x in xs for y in ys])
    return groups


HX, KX = (0, 1, 1, 0), (0, 0, 1, 1)
HY, KY, LY = (0, 1, 1, 0, 0, 1, 1, 0), (0, 0, 1, 0, 1, 1, 0, 1), (0, 0, 0, 1, 0, 1, 1, 1)


def place(core, u, v):
    return (u + 1 - core) % X * Y + (v + core) % Y


def route_groups(same, order):
    groups = []
    for core in range(CORE):
        found = {}
        for u in range(X):
            for v in range(Y):
                member = (order(u, v), core * X * Y + place(core, u, v))
                found.setdefault(same(u, v), []).append(member)
        groups += [[device for _, device in sorted(found[key])] for key in sorted(found)]
    return groups


def first_groups():
    return route_groups(lambda u, v: (u // 2, v // 2), lambda u, v: (HX[u], HY[v]))


def second_groups():
    return route_groups(lambda u, v: (HX[u], HY[v]), lambda u, v: (KX[u], KY[v], LY[v]))


def row_order(core):
    keys = []
    for u in range(X):
        for v in range(Y):
            keys.append(((HX[u], HY[v], KX[u], KY[v], LY[v]), place(core, u, v)))
    return [owner for _, owner in sorted(keys)]


def summed_exchange(array, groups):
    parts = array.reshape(len(groups[0]), array.shape[0] // len(groups[0]), array.shape[1])
    parts = lax.all_to_all(parts, PLANES, 0, 0, axis_index_groups=groups, tiled=True)
    return jnp.sum(parts.astype(jnp.float32), axis=0)


def near_exchange(array):
    return lax.all_to_all(
        array, PLANES, 0, 0, axis_index_groups=neighbour_blocks(), tiled=True
    )


def far_exchange(array):
    return lax.all_to_all(array, FAR, 0, 0, tiled=True)
UNROLL = 16


def pair_kernel(
    tile_ref, obs_ref, kind_ref, count_ref, core_ref, anom_ref, blocks_ref, taper_ref, out_ref,
    acc_ref, held_ref, sems, gain_ref,
):
    tiles, members, width = acc_ref.shape
    count = count_ref[0]
    steps = lax.div(count + (UNROLL - 1), UNROLL)

    y_copy = pltpu.make_async_copy(
        blocks_ref.at[:, 0:members], held_ref.at[:, 0:members], sems.at[0]
    )
    w_copy = pltpu.make_async_copy(
        blocks_ref.at[:, members : 2 * members], held_ref.at[:, members : 2 * members], sems.at[1]
    )
    y_copy.start()
    w_copy.start()

    @pl.loop(0, tiles, unroll=4)
    def _(t):
        acc_ref[t] = jnp.zeros((members, width), jnp.float32)

    y_copy.wait()

    @pl.loop(0, steps)
    def _(step):
        for u in range(UNROLL):
            q = step * UNROLL + u
            y = jnp.concatenate([held_ref[obs_ref[q], 0:128], held_ref[obs_ref[q], 128:256]], axis=1)
            start = pl.multiple_of(tile_ref[q] * width, width)
            anom = anom_ref[:, pl.ds(start, width)]
            cross = jnp.dot(y, anom, preferred_element_type=jnp.float32)
            gain = jnp.where(q < count, taper_ref[kind_ref[q]] * cross, 0.0)
            gain_ref[q] = gain.astype(jnp.bfloat16)

    w_copy.wait()

    @pl.loop(0, steps)
    def _(step):
        for u in range(UNROLL):
            q = step * UNROLL + u
            w = held_ref[obs_ref[q], members : 2 * members]
            acc_ref[tile_ref[q]] += jnp.dot(w, gain_ref[q], preferred_element_type=jnp.float32)

    rows = members // (X * Y)
    for core in range(CORE):
        order = row_order(core)

        @pl.when(core_ref[0] == core)
        def _():
            @pl.loop(0, tiles, unroll=2)
            def _(t):
                total = acc_ref[t]
                total = jnp.concatenate([total[rows * r : rows * (r + 1)] for r in order], axis=0)
                cells = pl.ds(pl.multiple_of(t * width, width), width)
                out_ref[:, cells] = total.astype(jnp.bfloat16)


def on_device(
    ensemble, obs_anom, obs_weight, taper_table, pair_obs, pair_tile, pair_taper, pair_count
):
    rows, cells = ensemble.shape
    members = rows * X * Y
    width = obs_anom.shape[1]
    tiles = cells // width
    pairs = pair_tile.shape[2]
    half = members // 2

    def reorder(array):
        split = array.reshape(XH, XL, YH, YL, rows, width)
        return split.transpose(1, 3, 0, 2, 4, 5).reshape(members, width)

    anomalies = reorder(obs_anom)
    blocks = jnp.concatenate(
        [anomalies[:half].T, anomalies[half:].T, obs_weight], axis=0
    )
    blocks = lax.all_gather(blocks, ("z", "core"), axis=0)
    part = far_exchange(jnp.broadcast_to(ensemble[None], (XH * YH, rows, cells)))
    part = part.reshape(1, XH * YH * rows, cells)
    panel = near_exchange(jnp.broadcast_to(part, (XL * YL, XH * YH * rows, cells)))
    panel = panel.reshape(members, cells).astype(jnp.float32)
    centre = jnp.sum(panel, axis=0, keepdims=True) * (1.0 / members)
    anom = (panel - centre).astype(jnp.bfloat16)
    tapers = jnp.swapaxes(taper_table, 1, 2) * (1.0 / (members - 1))
    smem = pl.BlockSpec(memory_space=pltpu.SMEM)
    vmem = pl.BlockSpec(memory_space=pltpu.VMEM)
    partial = pl.pallas_call(
        pair_kernel,
        out_shape=jax.ShapeDtypeStruct((members, cells), jnp.bfloat16),
        in_specs=[smem] * 5 + [vmem, pl.BlockSpec(memory_space=pltpu.HBM), vmem],
        out_specs=vmem,
        scratch_shapes=[
            pltpu.VMEM((tiles, members, width), jnp.float32),
            pltpu.VMEM(blocks.shape, jnp.bfloat16),
            pltpu.SemaphoreType.DMA((2,)),
            pltpu.VMEM((pairs, width, width), jnp.bfloat16),
        ],
        compiler_params=pltpu.CompilerParams(vmem_limit_bytes=47 * 2**20),
        name="pairs",
    )(
        pair_tile[0, 0], pair_obs[0, 0], pair_taper[0, 0], pair_count[0],
        lax.axis_index("core").reshape(1), anom, blocks, tapers,
    )
    summed = summed_exchange(partial, first_groups()).astype(jnp.bfloat16)
    update = summed_exchange(summed, second_groups())
    return (ensemble.astype(jnp.float32) + update).astype(jnp.bfloat16)


def solution(mesh):
    fine = Mesh(
        mesh.devices.reshape(Z, CORE, XH, XL, YH, YL), ("z", "core", "xh", "xl", "yh", "yl")
    )
    group, route = ("z", "core"), ("xh", "xl", "yh", "yl")
    placed = (
        P(route, group),
        P(None, group + route),
        P(None, group + route),
        P(),
        P(group, route, None),
        P(group, route, None),
        P(group, route, None),
        P(group, route),
    )
    return jax.shard_map(
        on_device, mesh=fine, in_specs=placed, out_specs=P(route, group), check_vma=False
    )
```

```python
import jax
import jax.numpy as jnp
from jax import lax
from jax.experimental import pallas as pl
from jax.experimental.pallas import tpu as pltpu
from jax.sharding import Mesh, PartitionSpec as P

Z, CORE, XH, XL, YH, YL = 12, 2, 2, 2, 4, 2
X, Y = XH * XL, YH * YL
FAR = ("xh", "yh")
PLANES = ("core", "xh", "xl", "yh", "yl")


def neighbour_blocks():
    groups = []
    for core in range(CORE):
        for bx in range(XH):
            for by in range(YH):
                xs = sorted(((2 * bx + core + a) % X for a in range(2)), key=lambda x: x % 2)
                ys = sorted(((2 * by + core + b) % Y for b in range(2)), key=lambda y: y % 2)
                groups.append([(core * X + x) * Y + y for x in xs for y in ys])
    return groups


HX, KX = (0, 1, 1, 0), (0, 0, 1, 1)
HY, KY, LY = (0, 1, 1, 0, 0, 1, 1, 0), (0, 0, 1, 0, 1, 1, 0, 1), (0, 0, 0, 1, 0, 1, 1, 1)


def place(core, u, v):
    return (u + 1 - core) % X * Y + (v + core) % Y


def route_groups(same, order):
    groups = []
    for core in range(CORE):
        found = {}
        for u in range(X):
            for v in range(Y):
                member = (order(u, v), core * X * Y + place(core, u, v))
                found.setdefault(same(u, v), []).append(member)
        groups += [[device for _, device in sorted(found[key])] for key in sorted(found)]
    return groups


def first_groups():
    return route_groups(lambda u, v: (u // 2, v // 2), lambda u, v: (HX[u], HY[v]))


def second_groups():
    return route_groups(
        lambda u, v: ((u + 1) % X // 2, (v + 1) % Y // 2), lambda u, v: (KX[u], KY[v])
    )


def third_groups():
    return route_groups(lambda u, v: (u, HY[v], KY[v]), lambda u, v: LY[v])


def row_order(core):
    keys = []
    for u in range(X):
        for v in range(Y):
            keys.append(((HX[u], HY[v], KX[u], KY[v], LY[v]), place(core, u, v)))
    return [owner for _, owner in sorted(keys)]


def summed_exchange(array, groups):
    parts = array.reshape(len(groups[0]), array.shape[0] // len(groups[0]), array.shape[1])
    parts = lax.all_to_all(parts, PLANES, 0, 0, axis_index_groups=groups, tiled=True)
    return jnp.sum(parts.astype(jnp.float32), axis=0)


def near_exchange(array):
    return lax.all_to_all(
        array, PLANES, 0, 0, axis_index_groups=neighbour_blocks(), tiled=True
    )


def far_exchange(array):
    return lax.all_to_all(array, FAR, 0, 0, tiled=True)
UNROLL = 32


def pair_kernel(
    tile_ref, obs_ref, kind_ref, count_ref, core_ref, anom_ref, blocks_ref, taper_ref, out_ref,
    acc_ref, held_ref, sems, gain_ref,
):
    tiles, members, width = acc_ref.shape
    count = count_ref[0]
    steps = lax.div(count + (UNROLL - 1), UNROLL)

    y_copy = pltpu.make_async_copy(
        blocks_ref.at[:, 0:members], held_ref.at[:, 0:members], sems.at[0]
    )
    w_copy = pltpu.make_async_copy(
        blocks_ref.at[:, members : 2 * members], held_ref.at[:, members : 2 * members], sems.at[1]
    )
    y_copy.start()
    w_copy.start()

    @pl.loop(0, tiles, unroll=4)
    def _(t):
        acc_ref[t] = jnp.zeros((members, width), jnp.float32)

    y_copy.wait()

    @pl.loop(0, steps)
    def _(step):
        for u in range(UNROLL):
            q = step * UNROLL + u
            y = jnp.concatenate([held_ref[obs_ref[q], 0:128], held_ref[obs_ref[q], 128:256]], axis=1)
            start = pl.multiple_of(tile_ref[q] * width, width)
            anom = anom_ref[:, pl.ds(start, width)]
            cross = jnp.dot(y, anom, preferred_element_type=jnp.float32)
            gain = jnp.where(q < count, taper_ref[kind_ref[q]] * cross, 0.0)
            gain_ref[q] = gain.astype(jnp.bfloat16)

    w_copy.wait()

    @pl.loop(0, steps)
    def _(step):
        for u in range(UNROLL):
            q = step * UNROLL + u
            w = held_ref[obs_ref[q], members : 2 * members]
            acc_ref[tile_ref[q]] += jnp.dot(w, gain_ref[q], preferred_element_type=jnp.float32)

    rows = members // (X * Y)
    for core in range(CORE):
        order = row_order(core)

        @pl.when(core_ref[0] == core)
        def _():
            @pl.loop(0, tiles, unroll=2)
            def _(t):
                total = acc_ref[t]
                total = jnp.concatenate([total[rows * r : rows * (r + 1)] for r in order], axis=0)
                cells = pl.ds(pl.multiple_of(t * width, width), width)
                out_ref[:, cells] = total.astype(jnp.bfloat16)


def on_device(
    ensemble, obs_anom, obs_weight, taper_table, pair_obs, pair_tile, pair_taper, pair_count
):
    rows, cells = ensemble.shape
    members = rows * X * Y
    width = obs_anom.shape[1]
    tiles = cells // width
    pairs = pair_tile.shape[2]
    half = members // 2

    def reorder(array):
        split = array.reshape(XH, XL, YH, YL, rows, width)
        return split.transpose(1, 3, 0, 2, 4, 5).reshape(members, width)

    anomalies = reorder(obs_anom)
    blocks = jnp.concatenate(
        [anomalies[:half].T, anomalies[half:].T, obs_weight], axis=0
    )
    blocks = lax.all_gather(blocks, ("z", "core"), axis=0)
    part = far_exchange(jnp.broadcast_to(ensemble[None], (XH * YH, rows, cells)))
    part = part.reshape(1, XH * YH * rows, cells)
    panel = near_exchange(jnp.broadcast_to(part, (XL * YL, XH * YH * rows, cells)))
    panel = panel.reshape(members, cells).astype(jnp.float32)
    centre = jnp.sum(panel, axis=0, keepdims=True) * (1.0 / members)
    anom = (panel - centre).astype(jnp.bfloat16)
    tapers = jnp.swapaxes(taper_table, 1, 2) * (1.0 / (members - 1))
    smem = pl.BlockSpec(memory_space=pltpu.SMEM)
    vmem = pl.BlockSpec(memory_space=pltpu.VMEM)
    partial = pl.pallas_call(
        pair_kernel,
        out_shape=jax.ShapeDtypeStruct((members, cells), jnp.bfloat16),
        in_specs=[smem] * 5 + [vmem, pl.BlockSpec(memory_space=pltpu.HBM), vmem],
        out_specs=vmem,
        scratch_shapes=[
            pltpu.VMEM((tiles, members, width), jnp.float32),
            pltpu.VMEM(blocks.shape, jnp.bfloat16),
            pltpu.SemaphoreType.DMA((2,)),
            pltpu.VMEM((pairs, width, width), jnp.bfloat16),
        ],
        compiler_params=pltpu.CompilerParams(vmem_limit_bytes=47 * 2**20),
        name="pairs",
    )(
        pair_tile[0, 0], pair_obs[0, 0], pair_taper[0, 0], pair_count[0],
        lax.axis_index("core").reshape(1), anom, blocks, tapers,
    )
    summed = summed_exchange(partial, first_groups()).astype(jnp.bfloat16)
    summed = summed_exchange(summed, second_groups()).astype(jnp.bfloat16)
    update = summed_exchange(summed, third_groups())
    return (ensemble.astype(jnp.float32) + update).astype(jnp.bfloat16)


def solution(mesh):
    fine = Mesh(
        mesh.devices.reshape(Z, CORE, XH, XL, YH, YL), ("z", "core", "xh", "xl", "yh", "yl")
    )
    group, route = ("z", "core"), ("xh", "xl", "yh", "yl")
    placed = (
        P(route, group),
        P(None, group + route),
        P(None, group + route),
        P(),
        P(group, route, None),
        P(group, route, None),
        P(group, route, None),
        P(group, route),
    )
    return jax.shard_map(
        on_device, mesh=fine, in_specs=placed, out_specs=P(route, group), check_vma=False
    )
```
